32 devices in a mesh: seq: 4 (over y, x), dp: 8 (over z, core).
Axes of the slice: x: 2, y: 2, z: 4, core: 2. Of those that a mesh axis runs over, the one named last changes fastest.
Arguments:
- tokens: bfloat16 [8, 2048, 768], P('dp', 'seq'), may hold values from -6 to 6
- ln_gain: bfloat16 [2, 768], P(None, 'dp'), may hold values from 0.5 to 1.5
- ln_bias: bfloat16 [2, 768], P(None, 'dp'), may hold values from -1.25 to 1.25
- w_qkv: bfloat16 [768, 2304], P('dp'), may hold values from -0.21875 to 0.21875
- qv_bias: bfloat16 [2, 768], P(None, 'dp'), may hold values from -1.25 to 1.25
- w_out: bfloat16 [768, 768], P('dp'), may hold values from -0.875 to 0.875
- w_fc: bfloat16 [768, 3072], P('dp'), may hold values from -0.21875 to 0.21875
- fc_bias: bfloat16 [3072], P('dp'), may hold values from -1.25 to 1.25
- w_proj: bfloat16 [3072, 768], P('dp'), may hold values from -0.109375 to 0.109375
- branch_bias: bfloat16 [2, 768], P(None, 'dp'), may hold values from -1.25 to 1.25
- cotangent: bfloat16 [8, 2048, 768], P('dp', 'seq'), may hold values from -8 to 8
Outputs:
- output: bfloat16 [8, 2048, 768], P('dp', 'seq')
- input_grad: bfloat16 [8, 2048, 768], P('dp', 'seq')
- grad_ln_gain: float32 [2, 768], P(None, 'dp')
- grad_ln_bias: float32 [2, 768], P(None, 'dp')
- grad_w_qkv: float32 [768, 2304], P('dp')
- grad_qv_bias: float32 [2, 768], P(None, 'dp')
- grad_w_out: float32 [768, 768], P('dp')
- grad_w_fc: float32 [768, 3072], P('dp')
- grad_fc_bias: float32 [3072], P('dp')
- grad_w_proj: float32 [3072, 768], P('dp')
- grad_branch_bias: float32 [2, 768], P(None, 'dp')
The draws below stay inside these ranges and needn't reach their ends.
All inputs are finite; a program needn't handle non-finite values.
Results may differ from the reference program's by a relative error of at most 0.013.
Values may be sent and summed in bfloat16 or wider, within the bound.
A program may use at most 128 MiB of HBM per device.

```python
import jax
import jax.numpy as jnp
from jax import lax

D = 768
HEADS = 12
HEAD_DIM = 64
FF = 3072
LEN = 2048
SEQUENCES = 8


def spiked(entries, key, source, target, shards_of, factor):
    def block_of(position):
        return (jnp.arange(entries.shape[position]) // (entries.shape[position] // shards_of)).reshape((-1,) + (1,) * (entries.ndim - 1 - position))

    one_side = jax.random.permutation(key, shards_of)[block_of(target)]
    second = (block_of(target) + shards_of // 2) % shards_of
    return jnp.where((block_of(source) == one_side) | (block_of(source) == second), factor * entries, entries)


def block_scale(rng, dims, cuts, smallest, high):
    gain = 1.0
    for position, blocks in cuts:
        heights = jax.random.uniform(jax.random.fold_in(jax.random.fold_in(rng, 6), position), (blocks,), jnp.float32, smallest / len(cuts), high / len(cuts))
        gain = gain * jnp.repeat(jnp.exp(heights), dims[position] // blocks).reshape((-1,) + (1,) * (len(dims) - 1 - position))
    return gain


def scatter_about(key, shape, deviation, reach, cuts=(), kind=jnp.bfloat16):
    gain = block_scale(key, shape, cuts, -0.22, 0.18) if cuts else 1.0
    values = jax.random.normal(key, shape, jnp.float32) * deviation * gain
    return jnp.minimum(jnp.maximum(values, -reach), reach).astype(kind)


def noise_with(own_key, shape, deviation, most, cuts, heavy, kind=jnp.bfloat16):
    array = deviation * jax.random.normal(own_key, shape, jnp.float32)
    if cuts:
        array = array * block_scale(own_key, shape, cuts, -0.22, 0.18)
    return jnp.clip(spiked(array, jax.random.fold_in(own_key, 3), *heavy), -most, most).astype(kind)


def setup_inputs(seed: int = 0) -> dict:
    keys = jax.random.split(jax.random.key(seed), 12)
    tokens = scatter_about(keys[0], (SEQUENCES, LEN, D), 1.0, 6.0, ((0, 8), (1, 4)))
    ln_gain = jnp.clip(1.0 + 0.1 * jax.random.normal(keys[1], (2, D), jnp.float32), 0.5, 1.5).astype(jnp.bfloat16)
    ln_bias = scatter_about(keys[2], (2, D), 0.2, 1.25, ((1, 8),))
    w_qkv = scatter_about(keys[3], (D, 3 * D), D ** -0.5, 0.21875, ((0, 8),))
    qv_bias = scatter_about(keys[4], (2, D), 0.2, 1.25, ((1, 8),))
    w_out = scatter_about(keys[5], (D, D), (D // 16) ** -0.5, 0.875, ((0, 8),))
    w_fc = scatter_about(keys[6], (D, FF), D ** -0.5, 0.21875, ((0, 8),))
    fc_bias = scatter_about(keys[7], (FF,), 0.2, 1.25, ((0, 8),))
    w_proj = scatter_about(keys[8], (FF, D), FF ** -0.5, 0.109375, ((0, 8),))
    branch_bias = scatter_about(keys[9], (2, D), 0.2, 1.25, ((1, 8),))
    cotangent = noise_with(keys[10], (SEQUENCES, LEN, D), 1.0, 8.0, ((0, 8), (1, 4)), (0, 2, 8, 2.0))
    return dict(tokens=tokens, ln_gain=ln_gain, ln_bias=ln_bias, w_qkv=w_qkv, qv_bias=qv_bias, w_out=w_out, w_fc=w_fc, fc_bias=fc_bias, w_proj=w_proj, branch_bias=branch_bias, cotangent=cotangent)


@jax.custom_vjp
def low(v):
    return lax.optimization_barrier(v.astype(jnp.bfloat16)).astype(jnp.float32)

@jax.custom_vjp
def low_back(v):
    return v

def low_keep(v):
    return (low(v), None)

def low_pass(kept, grad):
    return (grad,)

def back_keep(v):
    return (v, None)

def back_low(kept, grad):
    return (low(grad),)
low.defvjp(low_keep, low_pass)
low_back.defvjp(back_keep, back_low)
NORM_EPS = 1e-05
PRECISE = lax.Precision.HIGHEST

def layer_norm(vector, norm_gain, norm_shift):
    center = vector - lax.optimization_barrier(jnp.mean(vector, axis=-1, keepdims=True))
    spread = lax.optimization_barrier(jnp.mean(center * center, axis=-1, keepdims=True))
    return center * lax.rsqrt(spread + NORM_EPS) * norm_gain + norm_shift

def matmul(left_side, right_side):
    return jnp.dot(left_side, right_side, precision=PRECISE, preferred_element_type=jnp.float32)

def attention(queries, key_rows, values):
    block_rows = min(512, LEN)
    num_blocks = LEN // block_rows
    score_scale = HEAD_DIM ** (-0.5)
    head_queries = queries.reshape(LEN, HEADS, HEAD_DIM)
    head_keys = key_rows.reshape(LEN, HEADS, HEAD_DIM)
    head_values = values.reshape(LEN, HEADS, HEAD_DIM)
    positions = jnp.arange(LEN, dtype=jnp.int32)

    def one_block(block_index):
        start_row = (block_index * block_rows).astype(jnp.int32)
        query_block = lax.dynamic_slice_in_dim(head_queries, start_row, block_rows, 0)
        scores = jnp.einsum('qhd,khd->hqk', query_block, head_keys, precision=PRECISE) * score_scale
        row_places = start_row + jnp.arange(block_rows, dtype=jnp.int32)
        allowed = positions[None, :] <= row_places[:, None]
        scores = low_back(jnp.where(allowed[None], scores, -1e+30))
        weights = low(jax.nn.softmax(scores, axis=-1))
        return jnp.einsum('hqk,khd->qhd', weights, head_values, precision=PRECISE)
    block_outs = lax.map(jax.checkpoint(one_block), jnp.arange(num_blocks, dtype=jnp.int32))
    return block_outs.reshape(LEN, D)

def forward(source, ln_gain, ln_bias, w_qkv, qv_bias, w_out, w_fc, fc_bias, w_proj, branch_bias):
    normed_first = low(layer_norm(source, ln_gain[0], ln_bias[0]))
    projected = matmul(normed_first, w_qkv)
    queries = low_back(low(projected[:, :D] + qv_bias[0]))
    key_rows = low_back(low(projected[:, D:2 * D]))
    values = low_back(low(projected[:, 2 * D:] + qv_bias[1]))
    head_out = low_back(low(attention(queries, key_rows, values)))
    branch_attn = low_back(matmul(head_out, w_out) + branch_bias[0])
    middle = source + branch_attn
    second = low(layer_norm(middle, ln_gain[1], ln_bias[1]))
    hidden = low_back(matmul(second, w_fc) + fc_bias)
    active = low(jax.nn.gelu(hidden, approximate=True))
    return middle + (matmul(active, w_proj) + branch_bias[1])

def reference(tokens, ln_gain, ln_bias, w_qkv, qv_bias, w_out, w_fc, fc_bias, w_proj, branch_bias, cotangent):
    params = tuple((param.astype(jnp.float32) for param in (ln_gain, ln_bias, w_qkv, qv_bias, w_out, w_fc, fc_bias, w_proj, branch_bias)))
    zero_grads = tuple((jnp.zeros_like(param) for param in params))

    def per_sequence(totals, block_item):
        seq_input, seq_cotangent = block_item
        result, pullback = jax.vjp(forward, seq_input.astype(jnp.float32), *params)
        seq_grads = pullback(seq_cotangent.astype(jnp.float32))
        totals = tuple((total_sum + piece_sum for total_sum, piece_sum in zip(totals, seq_grads[1:])))
        return (totals, (result.astype(jnp.bfloat16), seq_grads[0].astype(jnp.bfloat16)))
    totals, (output, input_grad) = lax.scan(per_sequence, zero_grads, (tokens, cotangent))
    return (output, input_grad, totals[0], totals[1], totals[2], totals[3], totals[4], totals[5], totals[6], totals[7], totals[8])
```

```python
from functools import partial

import jax
import jax.numpy as jnp
from jax import lax
from jax.experimental import pallas as pl
from jax.experimental.pallas import tpu as pltpu
from jax.sharding import PartitionSpec as P

HEAD_DIM = 64
NORM_EPS = 1e-05
F32 = jnp.float32
BF16 = jnp.bfloat16
SCALE = HEAD_DIM ** (-0.5)


def layer_norm(vector, norm_gain, norm_shift):
    center = vector - jnp.mean(vector, axis=-1, keepdims=True)
    spread = jnp.mean(center * center, axis=-1, keepdims=True)
    return center * lax.rsqrt(spread + NORM_EPS) * norm_gain + norm_shift


def dot(left, right, left_dim, right_dim):
    return lax.dot_general(
        left, right, (((left_dim,), (right_dim,)), ((), ())), preferred_element_type=F32
    )


def causal(scores):
    keys = lax.broadcasted_iota(jnp.int32, scores.shape, 0)
    rows = lax.broadcasted_iota(jnp.int32, scores.shape, 1)
    return jnp.where(keys <= rows, scores, -1e30)


def forward_kernel(blocks, qkv_ref, out_ref, log_ref):
    for i in range(blocks):
        queries = qkv_ref[0, i] * BF16(SCALE)
        scores = [dot(qkv_ref[1, j], queries, 0, 0) for j in range(i + 1)]
        scores[i] = causal(scores[i])
        top = jnp.max(scores[0], axis=0, keepdims=True)
        for piece in scores[1:]:
            top = jnp.maximum(top, jnp.max(piece, axis=0, keepdims=True))
        total = 0.0
        mixed = 0.0
        for j in range(i + 1):
            weights = jnp.exp(scores[j] - top)
            total = total + jnp.sum(weights, axis=0, keepdims=True)
            mixed = mixed + dot(qkv_ref[2, j], weights.astype(BF16), 1, 0)
        out_ref[i] = (mixed / total).astype(BF16)
        log_ref[0, i] = jnp.broadcast_to(top + jnp.log(total), log_ref.shape[2:])


def backward_kernel(blocks, qkv_ref, out_ref, log_ref, grad_ref, result_ref, key_ref, value_ref):
    for i in range(blocks):
        queries = qkv_ref[0, i] * BF16(SCALE)
        grads = grad_ref[i]
        logs = log_ref[0, i, 0:1]
        spread = jnp.sum(grads.astype(F32) * out_ref[i].astype(F32), axis=0, keepdims=True)
        query_total = 0.0
        for j in range(i + 1):
            keys = qkv_ref[1, j]
            scores = dot(keys, queries, 0, 0)
            if j == i:
                scores = causal(scores)
            probs = jnp.exp(scores - logs)
            grad_probs = dot(qkv_ref[2, j], grads, 0, 0)
            grad_scores = (probs * (grad_probs - spread)).astype(BF16)
            query_total = query_total + dot(keys, grad_scores, 1, 0)
            key_part = dot(queries, grad_scores, 1, 1)
            value_part = dot(grads, probs.astype(BF16), 1, 1)
            if i == j:
                key_ref[j] = key_part
                value_ref[j] = value_part
            else:
                key_ref[j] += key_part
                value_ref[j] += value_part
        result_ref[0, i] = (query_total * SCALE).astype(BF16)
    for j in range(blocks):
        result_ref[1, j] = key_ref[j].astype(BF16)
        result_ref[2, j] = value_ref[j].astype(BF16)


def specs(blocks, rows):
    return (
        pl.BlockSpec((3, blocks, HEAD_DIM, rows), lambda h: (0, 0, h, 0)),
        pl.BlockSpec((blocks, HEAD_DIM, rows), lambda h: (0, h, 0)),
        pl.BlockSpec((1, blocks, 8, rows), lambda h: (h, 0, 0, 0)),
    )


def attend_forward(qkv):
    _, blocks, width, rows = qkv.shape
    heads = width // HEAD_DIM
    wide, narrow, log_spec = specs(blocks, rows)
    pairs = heads * rows * rows * blocks * (blocks + 1) // 2
    return pl.pallas_call(
        partial(forward_kernel, blocks),
        grid=(heads,),
        in_specs=[wide],
        out_specs=[narrow, log_spec],
        out_shape=[
            jax.ShapeDtypeStruct((blocks, width, rows), BF16),
            jax.ShapeDtypeStruct((heads, blocks, 8, rows), F32),
        ],
        compiler_params=pltpu.CompilerParams(vmem_limit_bytes=40 * 2**20),
        cost_estimate=pl.CostEstimate(
            flops=16 * pairs * HEAD_DIM, bytes_accessed=2 * qkv.size * 2, transcendentals=pairs
        ),
        name="attend_forward",
    )(qkv)


def attend_backward(qkv, out, logs, grads):
    _, blocks, width, rows = qkv.shape
    heads = width // HEAD_DIM
    wide, narrow, log_spec = specs(blocks, rows)
    pairs = heads * rows * rows * blocks * (blocks + 1) // 2
    return pl.pallas_call(
        partial(backward_kernel, blocks),
        grid=(heads,),
        in_specs=[wide, narrow, log_spec, narrow],
        out_specs=wide,
        out_shape=jax.ShapeDtypeStruct(qkv.shape, BF16),
        scratch_shapes=[
            pltpu.VMEM((blocks, HEAD_DIM, rows), F32),
            pltpu.VMEM((blocks, HEAD_DIM, rows), F32),
        ],
        compiler_params=pltpu.CompilerParams(vmem_limit_bytes=40 * 2**20),
        cost_estimate=pl.CostEstimate(
            flops=40 * pairs * HEAD_DIM, bytes_accessed=6 * qkv.size * 2, transcendentals=pairs
        ),
        name="attend_backward",
    )(qkv, out, logs, grads)


def swap(value, axis, bit):
    size = lax.axis_size(axis)
    return lax.ppermute(value, axis, [(d, d ^ bit) for d in range(size)])


def halve(value, axis, bit):
    mine = (lax.axis_index(axis) // bit) % 2
    value = value.reshape((value.shape[0] // 2, 2) + value.shape[1:])
    kept = lax.dynamic_index_in_dim(value, mine, 1, keepdims=False)
    sent = lax.dynamic_index_in_dim(value, 1 - mine, 1, keepdims=False)
    return kept.astype(F32) + swap(sent.astype(BF16), axis, bit).astype(F32)


def reduce_owned(value):
    owners = lax.axis_size("dp")
    parts = lax.axis_size("seq")
    rows = value.shape[0] // owners
    value = value.reshape((owners, parts, rows // parts) + value.shape[1:])
    value = halve(value, "dp", 1)
    place = lax.axis_index("seq")
    total = lax.dynamic_index_in_dim(value, place, 1, keepdims=False)
    for other in range(1, parts):
        sent = lax.dynamic_index_in_dim(value, place ^ other, 1, keepdims=False)
        total = total + swap(sent.astype(BF16), "seq", other).astype(F32)
    bit = 2
    while bit < owners:
        total = halve(total, "dp", bit)
        bit *= 2
    own = total[0].astype(BF16)
    return lax.all_gather(own, "seq", axis=0, tiled=True).astype(F32)


def shards(
    tokens, ln_gain, ln_bias, w_qkv, qv_bias, w_out, w_fc, fc_bias, w_proj, branch_bias, cotangent
):
    owners = lax.axis_size("dp")
    parts = lax.axis_size("seq")
    share = ln_gain.shape[1]
    width = share * owners
    packed = jnp.concatenate(
        [ln_gain, ln_bias, qv_bias, branch_bias, fc_bias.reshape(-1, share)], axis=0
    )
    vectors = lax.all_gather(packed, "dp", axis=1, tiled=True).astype(F32)
    full_qkv = lax.all_gather(w_qkv, "dp", axis=0, tiled=True)
    full_out = lax.all_gather(w_out, "dp", axis=0, tiled=True)
    full_fc = lax.all_gather(w_fc, "dp", axis=0, tiled=True)
    full_proj = lax.all_gather(w_proj, "dp", axis=0, tiled=True)
    gain_vals, shift_vals, qv_vals, branch_vals = (
        vectors[0:2], vectors[2:4], vectors[4:6], vectors[6:8],
    )
    fc_vals = vectors[8:].reshape(-1, owners, share).transpose(1, 0, 2).reshape(-1)
    source = tokens[0].astype(F32)
    rows = source.shape[0]
    normed_first = layer_norm(source, gain_vals[0], shift_vals[0]).astype(BF16)
    bias = jnp.concatenate([qv_vals[0], jnp.zeros((width,), F32), qv_vals[1]])
    projected = (dot(full_qkv, normed_first, 0, 1) + bias[:, None]).astype(BF16)
    projected = projected.reshape(3, parts, width // parts, rows)
    qkv = lax.all_to_all(projected, "seq", split_axis=1, concat_axis=1, tiled=True)
    seq_heads, logs = attend_forward(qkv)
    head_out = lax.all_to_all(seq_heads, "seq", split_axis=0, concat_axis=0, tiled=True)
    head_out = head_out.reshape(width, rows)
    middle = source + (dot(head_out, full_out, 0, 0) + branch_vals[0])
    second = layer_norm(middle, gain_vals[1], shift_vals[1]).astype(BF16)
    hidden = dot(second, full_fc, 1, 0) + fc_vals
    active = jax.nn.gelu(hidden, approximate=True).astype(BF16)
    result = middle + (dot(active, full_proj, 1, 0) + branch_vals[1])
    upstream = cotangent[0]
    upstream_vals = upstream.astype(F32)
    grad_proj_bias = jnp.sum(upstream_vals, axis=0)
    grad_active = dot(upstream, full_proj, 1, 1)
    _, gelu_back = jax.vjp(partial(jax.nn.gelu, approximate=True), hidden)
    grad_hidden = gelu_back(grad_active)[0].astype(BF16)
    grad_fc_bias = jnp.sum(grad_hidden.astype(F32), axis=0)
    grad_second = dot(grad_hidden, full_fc, 1, 1)
    _, second_back = jax.vjp(layer_norm, middle, gain_vals[1], shift_vals[1])
    middle_part, grad_gain_two, grad_shift_two = second_back(grad_second)
    grad_middle = upstream_vals + middle_part
    grad_branch = grad_middle.astype(BF16)
    grad_out_bias = jnp.sum(grad_branch.astype(F32), axis=0)
    grad_head_out = dot(full_out, grad_branch, 1, 1).astype(BF16)
    seq_grad = lax.all_to_all(
        grad_head_out.reshape(parts, width // parts, rows),
        "seq", split_axis=0, concat_axis=0, tiled=True,
    )
    grad_proj = dot(active, upstream, 0, 0)
    grad_fc = dot(second, grad_hidden, 0, 0)
    grad_out = dot(head_out, grad_branch, 1, 0)
    seq_dqkv = attend_backward(qkv, seq_heads, logs, seq_grad)
    grad_qkv = lax.all_to_all(seq_dqkv, "seq", split_axis=1, concat_axis=1, tiled=True)
    grad_projected = grad_qkv.reshape(3 * width, rows)
    grad_sums = jnp.sum(grad_projected.astype(F32), axis=1)
    grad_first = dot(grad_projected, full_qkv, 0, 1)
    grad_w_qkv = dot(normed_first, grad_projected, 0, 1)
    _, first_back = jax.vjp(layer_norm, source, gain_vals[0], shift_vals[0])
    source_part, grad_gain_one, grad_shift_one = first_back(grad_first)
    input_grad = (grad_middle + source_part).astype(BF16)
    small = jnp.concatenate(
        [
            jnp.stack(
                [
                    grad_gain_one, grad_gain_two, grad_shift_one, grad_shift_two,
                    grad_sums[:width], grad_sums[2 * width :], grad_out_bias, grad_proj_bias,
                ]
            ),
            grad_fc_bias.reshape(owners, -1, share).transpose(1, 0, 2).reshape(-1, width),
        ],
        axis=0,
    )
    small = lax.psum(small, ("dp", "seq"))
    small = lax.dynamic_slice_in_dim(small, lax.axis_index("dp") * share, share, 1)
    return (
        result.astype(BF16)[None],
        input_grad[None],
        small[0:2],
        small[2:4],
        reduce_owned(grad_w_qkv),
        small[4:6],
        reduce_owned(grad_out),
        reduce_owned(grad_fc),
        small[8:].reshape(-1),
        reduce_owned(grad_proj),
        small[6:8],
    )


def solution(mesh):
    placed = (
        P("dp", "seq", None),
        P(None, "dp"),
        P(None, "dp"),
        P("dp", None),
        P(None, "dp"),
        P("dp", None),
        P("dp", None),
        P("dp"),
        P("dp", None),
        P(None, "dp"),
        P("dp", "seq", None),
    )
    return jax.shard_map(
        shards,
        mesh=mesh,
        in_specs=placed,
        out_specs=(
            P("dp", "seq", None),
            P("dp", "seq", None),
            P(None, "dp"),
            P(None, "dp"),
            P("dp", None),
            P(None, "dp"),
            P("dp", None),
            P("dp", None),
            P("dp"),
            P("dp", None),
            P(None, "dp"),
        ),
        check_vma=False,
    )
```

```python
from functools import partial

import jax
import jax.numpy as jnp
from jax import lax
from jax.experimental import pallas as pl
from jax.experimental.pallas import tpu as pltpu
from jax.sharding import PartitionSpec as P

HEAD_DIM = 64
NORM_EPS = 1e-05
F32 = jnp.float32
BF16 = jnp.bfloat16
SCALE = HEAD_DIM ** (-0.5)


def layer_norm(vector, norm_gain, norm_shift):
    center = vector - jnp.mean(vector, axis=-1, keepdims=True)
    spread = jnp.mean(center * center, axis=-1, keepdims=True)
    return center * lax.rsqrt(spread + NORM_EPS) * norm_gain + norm_shift


def dot(left, right, left_dim, right_dim):
    return lax.dot_general(
        left, right, (((left_dim,), (right_dim,)), ((), ())), preferred_element_type=F32
    )


def causal(scores):
    keys = lax.broadcasted_iota(jnp.int32, scores.shape, 0)
    rows = lax.broadcasted_iota(jnp.int32, scores.shape, 1)
    return jnp.where(keys <= rows, scores, -1e30)


def forward_kernel(blocks, qkv_ref, out_ref, log_ref):
    for i in range(blocks):
        queries = qkv_ref[0, i] * BF16(SCALE)
        scores = [dot(qkv_ref[1, j], queries, 0, 0) for j in range(i + 1)]
        scores[i] = causal(scores[i])
        top = jnp.max(scores[0], axis=0, keepdims=True)
        for piece in scores[1:]:
            top = jnp.maximum(top, jnp.max(piece, axis=0, keepdims=True))
        total = 0.0
        mixed = 0.0
        for j in range(i + 1):
            weights = jnp.exp(scores[j] - top)
            total = total + jnp.sum(weights, axis=0, keepdims=True)
            mixed = mixed + dot(qkv_ref[2, j], weights.astype(BF16), 1, 0)
        out_ref[i] = (mixed / total).astype(BF16)
        log_ref[0, i] = jnp.broadcast_to(top + jnp.log(total), log_ref.shape[2:])


def backward_kernel(blocks, qkv_ref, out_ref, log_ref, grad_ref, result_ref, key_ref, value_ref):
    for i in range(blocks):
        queries = qkv_ref[0, i] * BF16(SCALE)
        grads = grad_ref[i]
        logs = log_ref[0, i, 0:1]
        spread = jnp.sum(grads.astype(F32) * out_ref[i].astype(F32), axis=0, keepdims=True)
        query_total = 0.0
        for j in range(i + 1):
            keys = qkv_ref[1, j]
            scores = dot(keys, queries, 0, 0)
            if j == i:
                scores = causal(scores)
            probs = jnp.exp(scores - logs)
            grad_probs = dot(qkv_ref[2, j], grads, 0, 0)
            grad_scores = (probs * (grad_probs - spread)).astype(BF16)
            query_total = query_total + dot(keys, grad_scores, 1, 0)
            key_part = dot(queries, grad_scores, 1, 1)
            value_part = dot(grads, probs.astype(BF16), 1, 1)
            if i == j:
                key_ref[j] = key_part
                value_ref[j] = value_part
            else:
                key_ref[j] += key_part
                value_ref[j] += value_part
        result_ref[0, i] = (query_total * SCALE).astype(BF16)
    for j in range(blocks):
        result_ref[1, j] = key_ref[j].astype(BF16)
        result_ref[2, j] = value_ref[j].astype(BF16)


def specs(blocks, rows):
    return (
        pl.BlockSpec((3, blocks, HEAD_DIM, rows), lambda h: (0, 0, h, 0)),
        pl.BlockSpec((blocks, HEAD_DIM, rows), lambda h: (0, h, 0)),
        pl.BlockSpec((1, blocks, 8, rows), lambda h: (h, 0, 0, 0)),
    )


def attend_forward(qkv):
    _, blocks, width, rows = qkv.shape
    heads = width // HEAD_DIM
    wide, narrow, log_spec = specs(blocks, rows)
    pairs = heads * rows * rows * blocks * (blocks + 1) // 2
    return pl.pallas_call(
        partial(forward_kernel, blocks),
        grid=(heads,),
        in_specs=[wide],
        out_specs=[narrow, log_spec],
        out_shape=[
            jax.ShapeDtypeStruct((blocks, width, rows), BF16),
            jax.ShapeDtypeStruct((heads, blocks, 8, rows), F32),
        ],
        compiler_params=pltpu.CompilerParams(vmem_limit_bytes=40 * 2**20),
        cost_estimate=pl.CostEstimate(
            flops=16 * pairs * HEAD_DIM, bytes_accessed=2 * qkv.size * 2, transcendentals=pairs
        ),
        name="attend_forward",
    )(qkv)


def attend_backward(qkv, out, logs, grads):
    _, blocks, width, rows = qkv.shape
    heads = width // HEAD_DIM
    wide, narrow, log_spec = specs(blocks, rows)
    pairs = heads * rows * rows * blocks * (blocks + 1) // 2
    return pl.pallas_call(
        partial(backward_kernel, blocks),
        grid=(heads,),
        in_specs=[wide, narrow, log_spec, narrow],
        out_specs=wide,
        out_shape=jax.ShapeDtypeStruct(qkv.shape, BF16),
        scratch_shapes=[
            pltpu.VMEM((blocks, HEAD_DIM, rows), F32),
            pltpu.VMEM((blocks, HEAD_DIM, rows), F32),
        ],
        compiler_params=pltpu.CompilerParams(vmem_limit_bytes=40 * 2**20),
        cost_estimate=pl.CostEstimate(
            flops=40 * pairs * HEAD_DIM, bytes_accessed=6 * qkv.size * 2, transcendentals=pairs
        ),
        name="attend_backward",
    )(qkv, out, logs, grads)


def swap(value, axis, bit):
    size = lax.axis_size(axis)
    return lax.ppermute(value, axis, [(d, d ^ bit) for d in range(size)])


def halve(value, axis, bit):
    mine = (lax.axis_index(axis) // bit) % 2
    value = value.reshape((value.shape[0] // 2, 2) + value.shape[1:])
    kept = lax.dynamic_index_in_dim(value, mine, 1, keepdims=False)
    sent = lax.dynamic_index_in_dim(value, 1 - mine, 1, keepdims=False)
    return kept.astype(F32) + swap(sent.astype(BF16), axis, bit).astype(F32)


def join(value, axis, bit, dim):
    upper = (lax.axis_index(axis) // bit) % 2 == 1
    other = swap(value, axis, bit)
    first = jnp.where(upper, other, value)
    second = jnp.where(upper, value, other)
    return jnp.stack([first, second], axis=dim)


def bits_of(axis):
    size = lax.axis_size(axis)
    bits = []
    bit = 1
    while bit < size:
        bits.insert(0, bit)
        bit *= 2
    return bits


def join_rows(value, axis, bits):
    for bit in bits:
        both = join(value, axis, bit, 1)
        value = both.reshape((-1,) + value.shape[1:])
    return value


def gather_small(value):
    return join_rows(value[None], "dp", bits_of("dp"))


def gather_rows(weight, flip):
    parts = lax.axis_size("seq")
    rows = weight.shape[0] // parts
    share = lax.dynamic_slice_in_dim(weight, lax.axis_index("seq") * rows, rows, 0)
    value = join_rows(share[None], "dp", bits_of("dp")[:-1])
    owners = value.shape[0]
    value = value[:, None]
    bits = bits_of("seq")
    for bit in bits[::-1] if flip else bits:
        both = join(value, "seq", bit, 1 if flip else 2)
        value = both.reshape((owners, -1) + value.shape[2:])
    value = value.reshape((owners, parts * rows) + weight.shape[1:])
    value = join_rows(value, "dp", [1])
    return value.reshape((-1,) + weight.shape[1:])


def reduce_first(value):
    owners = lax.axis_size("dp")
    parts = lax.axis_size("seq")
    rows = value.shape[0] // owners
    value = value.reshape((owners, parts, rows // parts) + value.shape[1:])
    return halve(value, "dp", 1)


def reduce_rest(value):
    owners = lax.axis_size("dp")
    parts = lax.axis_size("seq")
    place = lax.axis_index("seq")
    total = lax.dynamic_index_in_dim(value, place, 1, keepdims=False)
    for other in range(1, parts):
        sent = lax.dynamic_index_in_dim(value, place ^ other, 1, keepdims=False)
        total = total + swap(sent.astype(BF16), "seq", other).astype(F32)
    bit = 2
    while bit < owners:
        total = halve(total, "dp", bit)
        bit *= 2
    own = join_rows(total.astype(BF16), "seq", bits_of("seq"))
    return own.reshape((-1,) + own.shape[2:]).astype(F32)


def reduce_owned(value):
    return reduce_rest(reduce_first(value))


def shards(
    tokens, ln_gain, ln_bias, w_qkv, qv_bias, w_out, w_fc, fc_bias, w_proj, branch_bias, cotangent
):
    owners = lax.axis_size("dp")
    parts = lax.axis_size("seq")
    share = ln_gain.shape[1]
    width = share * owners
    packed = jnp.concatenate(
        [ln_gain, ln_bias, qv_bias, branch_bias, fc_bias.reshape(-1, share)], axis=0
    )
    lines = packed.shape[0]
    vectors = gather_small(packed).transpose(1, 0, 2).reshape(lines, -1).astype(F32)
    full_qkv = lax.all_gather(w_qkv, "dp", axis=0, tiled=True)
    full_out = lax.all_gather(w_out, "dp", axis=0, tiled=True)
    full_fc = gather_rows(w_fc, False)
    full_proj = gather_rows(w_proj, True)
    gain_vals, shift_vals, qv_vals, branch_vals = (
        vectors[0:2], vectors[2:4], vectors[4:6], vectors[6:8],
    )
    fc_vals = vectors[8:].reshape(-1, owners, share).transpose(1, 0, 2).reshape(-1)
    source = tokens[0].astype(F32)
    rows = source.shape[0]
    normed_first = layer_norm(source, gain_vals[0], shift_vals[0]).astype(BF16)
    bias = jnp.concatenate([qv_vals[0], jnp.zeros((width,), F32), qv_vals[1]])
    projected = (dot(full_qkv, normed_first, 0, 1) + bias[:, None]).astype(BF16)
    projected = projected.reshape(3, parts, width // parts, rows)
    qkv = lax.all_to_all(projected, "seq", split_axis=1, concat_axis=1, tiled=True)
    seq_heads, logs = attend_forward(qkv)
    head_out = lax.all_to_all(seq_heads, "seq", split_axis=0, concat_axis=0, tiled=True)
    head_out = head_out.reshape(width, rows)
    middle = source + (dot(head_out, full_out, 0, 0) + branch_vals[0])
    second = layer_norm(middle, gain_vals[1], shift_vals[1]).astype(BF16)
    hidden = dot(second, full_fc, 1, 0) + fc_vals
    active = jax.nn.gelu(hidden, approximate=True).astype(BF16)
    result = middle + (dot(active, full_proj, 1, 0) + branch_vals[1])
    upstream = cotangent[0]
    upstream_vals = upstream.astype(F32)
    grad_proj_bias = jnp.sum(upstream_vals, axis=0)
    grad_active = dot(upstream, full_proj, 1, 1)
    _, gelu_back = jax.vjp(partial(jax.nn.gelu, approximate=True), hidden)
    grad_hidden = gelu_back(grad_active)[0].astype(BF16)
    grad_fc_bias = jnp.sum(grad_hidden.astype(F32), axis=0)
    grad_second = dot(grad_hidden, full_fc, 1, 1)
    _, second_back = jax.vjp(layer_norm, middle, gain_vals[1], shift_vals[1])
    middle_part, grad_gain_two, grad_shift_two = second_back(grad_second)
    grad_middle = upstream_vals + middle_part
    grad_branch = grad_middle.astype(BF16)
    grad_out_bias = jnp.sum(grad_branch.astype(F32), axis=0)
    grad_head_out = dot(full_out, grad_branch, 1, 1).astype(BF16)
    seq_grad = lax.all_to_all(
        grad_head_out.reshape(parts, width // parts, rows),
        "seq", split_axis=0, concat_axis=0, tiled=True,
    )
    grad_proj = dot(active, upstream, 0, 0)
    grad_fc = dot(second, grad_hidden, 0, 0)
    grad_out = dot(head_out, grad_branch, 1, 0)
    early_proj, early_fc, seq_grad = lax.optimization_barrier(
        (reduce_first(grad_proj), reduce_first(grad_fc), seq_grad)
    )
    seq_dqkv = attend_backward(qkv, seq_heads, logs, seq_grad)
    grad_qkv = lax.all_to_all(seq_dqkv, "seq", split_axis=1, concat_axis=1, tiled=True)
    grad_projected = grad_qkv.reshape(3 * width, rows)
    grad_sums = jnp.sum(grad_projected.astype(F32), axis=1)
    grad_first = dot(grad_projected, full_qkv, 0, 1)
    grad_w_qkv = dot(normed_first, grad_projected, 0, 1)
    _, first_back = jax.vjp(layer_norm, source, gain_vals[0], shift_vals[0])
    source_part, grad_gain_one, grad_shift_one = first_back(grad_first)
    input_grad = (grad_middle + source_part).astype(BF16)
    small = jnp.concatenate(
        [
            jnp.stack(
                [
                    grad_gain_one, grad_gain_two, grad_shift_one, grad_shift_two,
                    grad_sums[:width], grad_sums[2 * width :], grad_out_bias, grad_proj_bias,
                ]
            ),
            grad_fc_bias.reshape(owners, -1, share).transpose(1, 0, 2).reshape(-1, width),
        ],
        axis=0,
    )
    small = small.reshape(lines, owners, share).transpose(1, 0, 2).reshape(-1, share)
    small = reduce_owned(small)
    return (
        result.astype(BF16)[None],
        input_grad[None],
        small[0:2],
        small[2:4],
        reduce_owned(grad_w_qkv),
        small[4:6],
        reduce_owned(grad_out),
        reduce_rest(early_fc),
        small[8:].reshape(-1),
        reduce_rest(early_proj),
        small[6:8],
    )


def solution(mesh):
    placed = (
        P("dp", "seq", None),
        P(None, "dp"),
        P(None, "dp"),
        P("dp", None),
        P(None, "dp"),
        P("dp", None),
        P("dp", None),
        P("dp"),
        P("dp", None),
        P(None, "dp"),
        P("dp", "seq", None),
    )
    return jax.shard_map(
        shards,
        mesh=mesh,
        in_specs=placed,
        out_specs=(
            P("dp", "seq", None),
            P("dp", "seq", None),
            P(None, "dp"),
            P(None, "dp"),
            P("dp", None),
            P(None, "dp"),
            P("dp", None),
            P("dp", None),
            P("dp"),
            P("dp", None),
            P(None, "dp"),
        ),
        check_vma=False,
    )
```

```python
from functools import partial

import jax
import jax.numpy as jnp
from jax import lax
from jax.experimental import pallas as pl
from jax.experimental.pallas import tpu as pltpu
from jax.sharding import PartitionSpec as P

HEAD_DIM = 64
NORM_EPS = 1e-05
F32 = jnp.float32
BF16 = jnp.bfloat16
SCALE = HEAD_DIM ** (-0.5)


def layer_norm(vector, norm_gain, norm_shift):
    center = vector - jnp.mean(vector, axis=-1, keepdims=True)
    spread = jnp.mean(center * center, axis=-1, keepdims=True)
    return center * lax.rsqrt(spread + NORM_EPS) * norm_gain + norm_shift


def dot(left, right, left_dim, right_dim):
    return lax.dot_general(
        left, right, (((left_dim,), (right_dim,)), ((), ())), preferred_element_type=F32
    )


def causal(scores):
    keys = lax.broadcasted_iota(jnp.int32, scores.shape, 0)
    rows = lax.broadcasted_iota(jnp.int32, scores.shape, 1)
    return jnp.where(keys <= rows, scores, -1e30)


def forward_kernel(blocks, qkv_ref, out_ref, log_ref):
    for i in range(blocks):
        queries = qkv_ref[0, i] * BF16(SCALE)
        scores = [dot(qkv_ref[1, j], queries, 0, 0) for j in range(i + 1)]
        scores[i] = causal(scores[i])
        top = jnp.max(scores[0], axis=0, keepdims=True)
        for piece in scores[1:]:
            top = jnp.maximum(top, jnp.max(piece, axis=0, keepdims=True))
        total = 0.0
        mixed = 0.0
        for j in range(i + 1):
            weights = jnp.exp(scores[j] - top)
            total = total + jnp.sum(weights, axis=0, keepdims=True)
            mixed = mixed + dot(qkv_ref[2, j], weights.astype(BF16), 1, 0)
        out_ref[i] = (mixed / total).astype(BF16)
        log_ref[0, i] = jnp.broadcast_to(top + jnp.log(total), log_ref.shape[2:])


def backward_kernel(blocks, qkv_ref, out_ref, log_ref, grad_ref, result_ref, key_ref, value_ref):
    for i in range(blocks):
        queries = qkv_ref[0, i] * BF16(SCALE)
        grads = grad_ref[i]
        logs = log_ref[0, i, 0:1]
        spread = jnp.sum(grads.astype(F32) * out_ref[i].astype(F32), axis=0, keepdims=True)
        query_total = 0.0
        for j in range(i + 1):
            keys = qkv_ref[1, j]
            scores = dot(keys, queries, 0, 0)
            if j == i:
                scores = causal(scores)
            probs = jnp.exp(scores - logs)
            grad_probs = dot(qkv_ref[2, j], grads, 0, 0)
            grad_scores = (probs * (grad_probs - spread)).astype(BF16)
            query_total = query_total + dot(keys, grad_scores, 1, 0)
            key_part = dot(queries, grad_scores, 1, 1)
            value_part = dot(grads, probs.astype(BF16), 1, 1)
            if i == j:
                key_ref[j] = key_part
                value_ref[j] = value_part
            else:
                key_ref[j] += key_part
                value_ref[j] += value_part
        result_ref[0, i] = (query_total * SCALE).astype(BF16)
    for j in range(blocks):
        result_ref[1, j] = key_ref[j].astype(BF16)
        result_ref[2, j] = value_ref[j].astype(BF16)


def specs(blocks, rows):
    return (
        pl.BlockSpec((3, blocks, HEAD_DIM, rows), lambda h: (0, 0, h, 0)),
        pl.BlockSpec((blocks, HEAD_DIM, rows), lambda h: (0, h, 0)),
        pl.BlockSpec((1, blocks, 8, rows), lambda h: (h, 0, 0, 0)),
    )


def attend_forward(qkv):
    _, blocks, width, rows = qkv.shape
    heads = width // HEAD_DIM
    wide, narrow, log_spec = specs(blocks, rows)
    pairs = heads * rows * rows * blocks * (blocks + 1) // 2
    return pl.pallas_call(
        partial(forward_kernel, blocks),
        grid=(heads,),
        in_specs=[wide],
        out_specs=[narrow, log_spec],
        out_shape=[
            jax.ShapeDtypeStruct((blocks, width, rows), BF16),
            jax.ShapeDtypeStruct((heads, blocks, 8, rows), F32),
        ],
        compiler_params=pltpu.CompilerParams(vmem_limit_bytes=40 * 2**20),
        cost_estimate=pl.CostEstimate(
            flops=16 * pairs * HEAD_DIM, bytes_accessed=2 * qkv.size * 2, transcendentals=pairs
        ),
        name="attend_forward",
    )(qkv)


def attend_backward(qkv, out, logs, grads):
    _, blocks, width, rows = qkv.shape
    heads = width // HEAD_DIM
    wide, narrow, log_spec = specs(blocks, rows)
    pairs = heads * rows * rows * blocks * (blocks + 1) // 2
    return pl.pallas_call(
        partial(backward_kernel, blocks),
        grid=(heads,),
        in_specs=[wide, narrow, log_spec, narrow],
        out_specs=wide,
        out_shape=jax.ShapeDtypeStruct(qkv.shape, BF16),
        scratch_shapes=[
            pltpu.VMEM((blocks, HEAD_DIM, rows), F32),
            pltpu.VMEM((blocks, HEAD_DIM, rows), F32),
        ],
        compiler_params=pltpu.CompilerParams(vmem_limit_bytes=40 * 2**20),
        cost_estimate=pl.CostEstimate(
            flops=40 * pairs * HEAD_DIM, bytes_accessed=6 * qkv.size * 2, transcendentals=pairs
        ),
        name="attend_backward",
    )(qkv, out, logs, grads)


def swap(value, axis, bit):
    size = lax.axis_size(axis)
    return lax.ppermute(value, axis, [(d, d ^ bit) for d in range(size)])


def halve(value, axis, bit):
    mine = (lax.axis_index(axis) // bit) % 2
    value = value.reshape((value.shape[0] // 2, 2) + value.shape[1:])
    kept = lax.dynamic_index_in_dim(value, mine, 1, keepdims=False)
    sent = lax.dynamic_index_in_dim(value, 1 - mine, 1, keepdims=False)
    return kept.astype(F32) + swap(sent.astype(BF16), axis, bit).astype(F32)


def join(value, axis, bit, dim):
    upper = (lax.axis_index(axis) // bit) % 2 == 1
    other = swap(value, axis, bit)
    first = jnp.where(upper, other, value)
    second = jnp.where(upper, value, other)
    return jnp.stack([first, second], axis=dim)


def bits_of(axis):
    size = lax.axis_size(axis)
    bits = []
    bit = 1
    while bit < size:
        bits.insert(0, bit)
        bit *= 2
    return bits


def join_rows(value, axis, bits):
    for bit in bits:
        both = join(value, axis, bit, 1)
        value = both.reshape((-1,) + value.shape[1:])
    return value


def gather_small(value):
    return join_rows(value[None], "dp", bits_of("dp"))


def together(*values):
    return lax.optimization_barrier(values)


def gather_far(weight):
    parts = lax.axis_size("seq")
    rows = weight.shape[0] // parts
    share = lax.dynamic_slice_in_dim(weight, lax.axis_index("seq") * rows, rows, 0)
    return join_rows(share[None], "dp", bits_of("dp")[:-1])


def gather_core(value):
    value = join_rows(value, "dp", [1])
    return value.reshape((-1,) + value.shape[2:])


def reduce_first(value):
    owners = lax.axis_size("dp")
    parts = lax.axis_size("seq")
    rows = value.shape[0] // owners
    value = value.reshape((owners, parts, rows // parts) + value.shape[1:])
    return halve(value, "dp", 1)


def reduce_seq(value):
    parts = lax.axis_size("seq")
    place = lax.axis_index("seq")
    total = lax.dynamic_index_in_dim(value, place, 1, keepdims=False)
    for other in range(1, parts):
        sent = lax.dynamic_index_in_dim(value, place ^ other, 1, keepdims=False)
        total = total + swap(sent.astype(BF16), "seq", other).astype(F32)
    return total


def reduce_far(total):
    owners = lax.axis_size("dp")
    if owners > 8:
        bit = 2
        while bit < owners:
            total = halve(total, "dp", bit)
            bit *= 2
        return total[0]
    far = lax.axis_index("dp") // 2
    kept = lax.dynamic_index_in_dim(total, far, 0, keepdims=False)
    for other in range(1, owners // 2):
        sent = lax.dynamic_index_in_dim(total, far ^ other, 0, keepdims=False)
        kept = kept + swap(sent.astype(BF16), "dp", 2 * other).astype(F32)
    return kept


def gather_seq(own):
    own = own.astype(BF16)
    parts = lax.axis_size("seq")
    pieces = [own] + [swap(own, "seq", other) for other in range(1, parts)]
    bit = 1
    while bit < parts:
        upper = (lax.axis_index("seq") // bit) % 2 == 1
        pieces = [jnp.where(upper, pieces[k ^ bit], pieces[k]) for k in range(parts)]
        bit *= 2
    return jnp.stack(pieces).astype(F32)


def flat(value):
    return value.reshape((-1,) + value.shape[2:])


def shards(
    tokens, ln_gain, ln_bias, w_qkv, qv_bias, w_out, w_fc, fc_bias, w_proj, branch_bias, cotangent
):
    owners = lax.axis_size("dp")
    parts = lax.axis_size("seq")
    share = ln_gain.shape[1]
    width = share * owners
    packed = jnp.concatenate(
        [ln_gain, ln_bias, qv_bias, branch_bias, fc_bias.reshape(-1, share)], axis=0
    )
    lines = packed.shape[0]
    vectors = gather_small(packed).transpose(1, 0, 2).reshape(lines, -1).astype(F32)
    full_qkv = lax.all_gather(w_qkv, "dp", axis=0, tiled=True)
    full_out = lax.all_gather(w_out, "dp", axis=0, tiled=True)
    full_fc = lax.all_gather(w_fc, "dp", axis=0, tiled=True)
    far_proj = gather_far(w_proj)
    full_qkv, far_proj, vectors = together(full_qkv, far_proj, vectors)
    gain_vals, shift_vals, qv_vals, branch_vals = (
        vectors[0:2], vectors[2:4], vectors[4:6], vectors[6:8],
    )
    fc_vals = vectors[8:].reshape(-1, owners, share).transpose(1, 0, 2).reshape(-1)
    source = tokens[0].astype(F32)
    rows = source.shape[0]
    normed_first = layer_norm(source, gain_vals[0], shift_vals[0]).astype(BF16)
    bias = jnp.concatenate([qv_vals[0], jnp.zeros((width,), F32), qv_vals[1]])
    projected = (dot(full_qkv, normed_first, 0, 1) + bias[:, None]).astype(BF16)
    projected = projected.reshape(3, parts, width // parts, rows)
    qkv = lax.all_to_all(projected, "seq", split_axis=1, concat_axis=1, tiled=True)
    qkv, far_proj = together(qkv, far_proj)
    near_proj = join(far_proj, "seq", 1, 1)
    near_proj = near_proj.reshape((near_proj.shape[0], -1) + near_proj.shape[3:])
    seq_heads, logs = attend_forward(qkv)
    seq_heads, logs, near_proj = together(seq_heads, logs, near_proj)
    head_out = lax.all_to_all(seq_heads, "seq", split_axis=0, concat_axis=0, tiled=True)
    head_out = head_out.reshape(width, rows)
    bit = 2
    while bit < parts:
        near_proj = join(near_proj, "seq", bit, 1)
        near_proj = near_proj.reshape((near_proj.shape[0], -1) + near_proj.shape[3:])
        bit *= 2
    head_out, near_proj = together(head_out, near_proj)
    full_proj = gather_core(near_proj)
    middle = source + (dot(head_out, full_out, 0, 0) + branch_vals[0])
    second = layer_norm(middle, gain_vals[1], shift_vals[1]).astype(BF16)
    hidden = dot(second, full_fc, 1, 0) + fc_vals
    active = jax.nn.gelu(hidden, approximate=True).astype(BF16)
    result = middle + (dot(active, full_proj, 1, 0) + branch_vals[1])
    upstream = cotangent[0]
    upstream_vals = upstream.astype(F32)
    grad_proj_bias = jnp.sum(upstream_vals, axis=0)
    grad_active = dot(upstream, full_proj, 1, 1)
    _, gelu_back = jax.vjp(partial(jax.nn.gelu, approximate=True), hidden)
    grad_hidden = gelu_back(grad_active)[0].astype(BF16)
    grad_fc_bias = jnp.sum(grad_hidden.astype(F32), axis=0)
    grad_second = dot(grad_hidden, full_fc, 1, 1)
    _, second_back = jax.vjp(layer_norm, middle, gain_vals[1], shift_vals[1])
    middle_part, grad_gain_two, grad_shift_two = second_back(grad_second)
    grad_middle = upstream_vals + middle_part
    grad_branch = grad_middle.astype(BF16)
    grad_out_bias = jnp.sum(grad_branch.astype(F32), axis=0)
    grad_head_out = dot(full_out, grad_branch, 1, 1).astype(BF16)
    seq_grad = lax.all_to_all(
        grad_head_out.reshape(parts, width // parts, rows),
        "seq", split_axis=0, concat_axis=0, tiled=True,
    )
    grad_proj = dot(active, upstream, 0, 0)
    grad_fc = dot(second, grad_hidden, 0, 0)
    grad_out = dot(head_out, grad_branch, 1, 0)
    early_proj, early_fc, seq_grad = lax.optimization_barrier(
        (reduce_first(grad_proj), reduce_first(grad_fc), seq_grad)
    )
    early_proj = reduce_seq(early_proj)
    early_fc = reduce_seq(early_fc)
    seq_dqkv = attend_backward(qkv, seq_heads, logs, seq_grad)
    seq_dqkv, early_proj, early_fc = together(seq_dqkv, early_proj, early_fc)
    grad_qkv = lax.all_to_all(seq_dqkv, "seq", split_axis=1, concat_axis=1, tiled=True)
    grad_projected = grad_qkv.reshape(3 * width, rows)
    grad_sums = jnp.sum(grad_projected.astype(F32), axis=1)
    grad_first = dot(grad_projected, full_qkv, 0, 1)
    grad_w_qkv = dot(normed_first, grad_projected, 0, 1)
    _, first_back = jax.vjp(layer_norm, source, gain_vals[0], shift_vals[0])
    source_part, grad_gain_one, grad_shift_one = first_back(grad_first)
    input_grad = (grad_middle + source_part).astype(BF16)
    small = jnp.concatenate(
        [
            jnp.stack(
                [
                    grad_gain_one, grad_gain_two, grad_shift_one, grad_shift_two,
                    grad_sums[:width], grad_sums[2 * width :], grad_out_bias, grad_proj_bias,
                ]
            ),
            grad_fc_bias.reshape(owners, -1, share).transpose(1, 0, 2).reshape(-1, width),
        ],
        axis=0,
    )
    count = lines * share // parts
    small = small.reshape(lines, owners, share).transpose(1, 0, 2).reshape(owners, parts, 1, count)
    small = jnp.pad(small, ((0, 0), (0, 0), (0, 7), (0, width - count)))
    bundle = jnp.concatenate([grad_out.reshape(owners, parts, -1, width), small], axis=2)
    bundle = reduce_first(bundle.reshape(-1, width))
    first_qkv = reduce_first(grad_w_qkv)
    bundle = gather_seq(reduce_far(reduce_seq(bundle)))
    sum_qkv = flat(gather_seq(reduce_far(reduce_seq(first_qkv))))
    sum_out = flat(bundle[:, :-8])
    small = bundle[:, -8, :count].reshape(lines, share)
    return (
        result.astype(BF16)[None],
        input_grad[None],
        small[0:2],
        small[2:4],
        sum_qkv,
        small[4:6],
        sum_out,
        flat(gather_seq(reduce_far(early_fc))),
        small[8:].reshape(-1),
        flat(gather_seq(reduce_far(early_proj))),
        small[6:8],
    )


def solution(mesh):
    placed = (
        P("dp", "seq", None),
        P(None, "dp"),
        P(None, "dp"),
        P("dp", None),
        P(None, "dp"),
        P("dp", None),
        P("dp", None),
        P("dp"),
        P("dp", None),
        P(None, "dp"),
        P("dp", "seq", None),
    )
    return jax.shard_map(
        shards,
        mesh=mesh,
        in_specs=placed,
        out_specs=(
            P("dp", "seq", None),
            P("dp", "seq", None),
            P(None, "dp"),
            P(None, "dp"),
            P("dp", None),
            P(None, "dp"),
            P("dp", None),
            P("dp", None),
            P("dp"),
            P("dp", None),
            P(None, "dp"),
        ),
        check_vma=False,
    )
```
